32 devices in a mesh: level: 4 (over y, x), gx: 4 (over z), gy: 2 (over core).
Axes of the slice: x: 2, y: 2, z: 4, core: 2. Of those that a mesh axis runs over, the one named last changes fastest.
Arguments:
- state: float32 [5, 32, 32, 128], P(None, 'gx', 'gy'), may hold values from -0.75 to 5.3, as said below
Outputs:
- level_states: float32 [4, 5, 32, 32, 128], P('level', None, 'gx', 'gy')
The draws below stay inside these ranges and needn't reach their ends.
Inputs may be any that keep to these rules, and one draw needn't show every extreme that they name: state[0] is a density from 1.5 to 3; state[1:4] are the density times velocity components, each velocity component of magnitude at most 0.25; state[4] is the total energy, a pressure from 1 to 2 divided by 0.4 plus the kinetic energy.
All inputs are finite; a program needn't handle non-finite values.
Results may differ from the reference program's by a relative error of at most 0.0001.
Values sent between devices are 32-bit elements; how exact they have to be, the bound alone decides.
No kernel may reach another device: no remote copies, remote signals or barrier semaphores. Data moves between devices by JAX's collectives and lax.ppermute only.
A program may use at most 64 MiB of HBM per device.

```python
import math
import jax
import jax.numpy as jnp

NZ = 128
STEPS = 3
NX = 32
NY = 32
N_LEVEL = 4


def draw_state(key, part):
    keys = jax.random.split(jax.random.fold_in(key, 17), 3)
    shape = (NX, NY, NZ)
    specific_volume_inverse = jnp.exp(jax.random.uniform(keys[0], shape, jnp.float32, math.log(1.5), math.log(3.0)))
    normal_stress_scalar = jax.random.uniform(keys[1], shape, jnp.float32, 1.0, 2.0)
    velocity = jax.random.uniform(keys[2], (3,) + shape, jnp.float32, -0.25, 0.25)
    momentum = specific_volume_inverse[None] * velocity
    energy = normal_stress_scalar / 0.4 + 0.5 * specific_volume_inverse * jnp.sum(velocity * velocity, axis=0)
    return jnp.concatenate([specific_volume_inverse[None], momentum, energy[None]], axis=0).astype(jnp.float32)


def setup_inputs(seed: int = 0) -> dict:
    splits = jax.random.split(jax.random.key(seed), 2)
    return {
        "state": draw_state(jax.random.fold_in(splits[1], 71), 0),
    }


DT = 0.1
GAMMA = 1.4
SHEAR_COEFFICIENT = 0.1
CONDUCTIVITY = 0.1
FIRST_COEF = (4.0 / 5.0, -1.0 / 5.0, 4.0 / 105.0, -1.0 / 280.0)
SECOND_CENTER = -205.0 / 72.0
SECOND_COEF = (8.0 / 5.0, -1.0 / 5.0, 8.0 / 315.0, -1.0 / 560.0)


def shifted(quantity, direction, offset):
    extent = quantity.shape[-3:]
    picks = [slice(4, extent[0] - 4), slice(4, extent[1] - 4), slice(4, extent[2] - 4)]
    picks[direction] = slice(4 + offset, extent[direction] - 4 + offset)
    leading = (slice(None),) * (quantity.ndim - 3)
    return quantity[leading + tuple(picks)]


def first_derivative(quantity, direction):
    total = 0.0
    for position, weight in enumerate(FIRST_COEF):
        total = total + weight * (shifted(quantity, direction, position + 1) - shifted(quantity, direction, -position - 1))
    return total


def second_derivative_sum(quantity):
    total = 0.0
    for direction in range(3):
        total = total + SECOND_CENTER * shifted(quantity, direction, 0)
        for position, weight in enumerate(SECOND_COEF):
            total = total + weight * (shifted(quantity, direction, position + 1) + shifted(quantity, direction, -position - 1))
    return total


def tendency(padded):
    specific_volume_inverse = padded[0]
    momentum = padded[1:4]
    energy = padded[4]
    velocity = momentum / specific_volume_inverse
    kinetic_energy_share = 0.5 * jnp.sum(velocity * velocity, axis=0)
    normal_stress_scalar = (GAMMA - 1.0) * (energy - specific_volume_inverse * kinetic_energy_share)
    absolute_kelvin_value = normal_stress_scalar / specific_volume_inverse
    divergence = 0.0
    for direction in range(3):
        along = velocity[direction]
        rows = [momentum[component] * along + (normal_stress_scalar if component == direction else 0.0) for component in range(3)]
        flux = jnp.stack([momentum[direction]] + rows + [(energy + normal_stress_scalar) * along])
        divergence = divergence + first_derivative(flux, direction)
    viscous = SHEAR_COEFFICIENT * second_derivative_sum(velocity)
    conduction_contribution = SHEAR_COEFFICIENT * second_derivative_sum(kinetic_energy_share) + CONDUCTIVITY * second_derivative_sum(absolute_kelvin_value)
    return jnp.concatenate([-divergence[0:1], viscous - divergence[1:4], (conduction_contribution - divergence[4])[None]], axis=0)


def reference(state):
    finals = []
    history = None
    for level_number in range(N_LEVEL):
        nodes = STEPS + 1 if level_number < N_LEVEL - 1 else STEPS
        current = state
        record = []
        for node in range(nodes):
            padded = jnp.pad(current, ((0, 0), (4, 4), (4, 4), (4, 4)), mode="wrap")
            forcing = tendency(padded)
            record.append(forcing)
            if node < STEPS:
                if history is None:
                    current = current + DT * forcing
                else:
                    if node == 0:
                        quad_term = 0.5 * (history[0] + history[1])
                    else:
                        quad_term = (8.0 * history[node] + 5.0 * history[node + 1] - history[node - 1]) / 12.0
                    current = current + DT * (forcing - history[node] + quad_term)
        finals.append(current)
        history = record
    return jnp.stack(finals)
```

```python
import functools

import jax
import jax.numpy as jnp
import ml_dtypes
import numpy as np
from jax import lax
from jax.experimental import pallas as pl
from jax.experimental.pallas import tpu as pltpu
from jax.sharding import PartitionSpec as P

STEPS = 3


DT = 0.1
GAMMA = 1.4
SHEAR_COEFFICIENT = 0.1
CONDUCTIVITY = 0.1
FIRST_COEF = (4.0 / 5.0, -1.0 / 5.0, 4.0 / 105.0, -1.0 / 280.0)
SECOND_CENTER = -205.0 / 72.0
SECOND_COEF = (8.0 / 5.0, -1.0 / 5.0, 8.0 / 315.0, -1.0 / 560.0)
REACH = 4
SCALE = 5040
FIRST_WHOLE = tuple(round(w * SCALE) for w in FIRST_COEF)
SECOND_WHOLE = tuple(round(w * SCALE) for w in SECOND_COEF)
VMEM_BUDGET = 56 * 1024 * 1024


def circulants(extent):
    first = np.zeros((extent, extent), np.float32)
    second = np.zeros((extent, extent), np.float32)
    for place in range(extent):
        for k in range(1, REACH + 1):
            first[place, (place + k) % extent] -= FIRST_WHOLE[k - 1]
            first[place, (place - k) % extent] += FIRST_WHOLE[k - 1]
            second[place, (place + k) % extent] += SECOND_WHOLE[k - 1]
            second[place, (place - k) % extent] += SECOND_WHOLE[k - 1]
    return first, second


def split(value):
    high = value.astype(jnp.bfloat16)
    low = (value - high.astype(jnp.float32)).astype(jnp.bfloat16)
    return high, low


def levels_kernel(rows, where, *refs):
    n_pieces = (len(refs) - 4 - 16) // 2
    mine, theirs = refs[:n_pieces], refs[n_pieces : 2 * n_pieces]
    wz_first, wz_second, wy, out = refs[2 * n_pieces : 2 * n_pieces + 4]
    base, fx, vis, part, G0, A1, A2, B1, A3, B2, C1, B3, C2, D1, C3, D2 = refs[2 * n_pieces + 4 :]
    fields, X, Y, Z = base.shape
    half = mine[0].shape[2]
    level, side = where[0], where[1]
    own = (X - rows) // 2

    starts = []
    place = own
    for piece in range(n_pieces):
        starts.append((own + piece * rows) % X)
    for group, core in ((mine, side), (theirs, 1 - side)):
        at = pl.multiple_of(core * half, half)
        for start, ref in zip(starts, group):
            fit = min(rows, X - start)
            base[:, start : start + fit, pl.ds(at, half), :] = ref[:, :fit]
            if fit < rows:
                base[:, : rows - fit, pl.ds(at, half), :] = ref[:, fit:]

    def pointwise(u):
        rho, m0, m1, m2, energy = u
        inverse = 1.0 / rho
        v0, v1, v2 = m0 * inverse, m1 * inverse, m2 * inverse
        m00, m11, m22 = m0 * v0, m1 * v1, m2 * v2
        m01, m02, m12 = m0 * v1, m0 * v2, m1 * v2
        twice = m00 + m11 + m22
        p = (GAMMA - 1.0) * energy - (0.5 * (GAMMA - 1.0)) * twice
        heat = energy + p
        warm = inverse * ((0.5 * SHEAR_COEFFICIENT) * twice + CONDUCTIVITY * p)
        s = SHEAR_COEFFICIENT
        g = [s * v0, s * v1, s * v2, warm]
        along_x = [m0, m00 + p, m01, m02, heat * v0]
        along_y = [m1, m01, m11 + p, m12, heat * v1]
        along_z = [m2, m02, m12, m22 + p, heat * v2]
        return along_x, along_y, along_z, g

    def flux_rows(make, first, count, whole):
        batch = 2

        def step(i, carry):
            x = first + i * batch
            u = [make(f, x, batch).reshape(batch * Y, Z) for f in range(fields)]
            along_x, along_y, along_z, g = pointwise(u)
            for f in range(fields):
                fx[f, pl.ds(x + REACH, batch)] = along_x[f].reshape(batch, Y, Z)
            for f in range(fields - 1):
                vis[f, pl.ds(x + REACH, batch)] = g[f].reshape(batch, Y, Z)
            if whole:
                gs = [split(v) for v in g]
                zs = [split(v) for v in along_z]
                ys = [split(v) for v in along_y]
                flux = jnp.concatenate([jnp.concatenate(pair, axis=1) for pair in zs], axis=0)
                flux = jnp.dot(flux, wz_first[...], preferred_element_type=jnp.float32)
                soft = jnp.concatenate([jnp.concatenate(pair, axis=1) for pair in gs], axis=0)
                soft = jnp.dot(soft, wz_second[...], preferred_element_type=jnp.float32)
                zero = jnp.zeros((Y, Z), jnp.bfloat16)
                for r in range(batch):
                    cut = slice(r * Y, (r + 1) * Y)
                    columns = []
                    for f in range(fields):
                        pair = [v[cut] for v in gs[f - 1]] if f else [zero, zero]
                        columns.append(jnp.concatenate([v[cut] for v in ys[f]] + pair, axis=0))
                    deep = jnp.dot(wy[...], jnp.concatenate(columns, axis=1), preferred_element_type=jnp.float32)
                    for f in range(fields):
                        total = deep[:, f * Z : (f + 1) * Z]
                        at = f * batch * Y + r * Y
                        total = total + flux[at : at + Y]
                        if f:
                            at = (f - 1) * batch * Y + r * Y
                            total = total + soft[at : at + Y]
                        part[f, x + r] = total
            return carry

        lax.fori_loop(0, count // batch, step, 0)

    def stencil_rows(target, shift, first, count, y_first, y_count):
        block, tile = 8, 8
        across = y_count // tile

        def step(i, carry):
            x = first + (i // across) * block
            y = pl.multiple_of(y_first + (i % across) * tile, tile)
            for f in range(fields):
                flux = fx[f, pl.ds(x, block + 2 * REACH), pl.ds(y, tile), :]
                total = part[f, pl.ds(x, block), pl.ds(y, tile), :]
                if f:
                    g = vis[f - 1, pl.ds(x, block + 2 * REACH), pl.ds(y, tile), :]
                    total = total + (3 * SECOND_CENTER * SCALE) * g[REACH : REACH + block]
                for k in range(1, REACH + 1):
                    ahead = slice(REACH + k, REACH + k + block)
                    behind = slice(REACH - k, REACH - k + block)
                    total = total + float(FIRST_WHOLE[k - 1]) * (flux[behind] - flux[ahead])
                    if f:
                        total = total + float(SECOND_WHOLE[k - 1]) * (g[behind] + g[ahead])
                target[f, pl.ds(x - shift, block), pl.ds(y, tile), :] = (DT / SCALE) * total
            return carry

        lax.fori_loop(0, (count // block) * across, step, 0)

    def tendency(target, make, reach, last=False):
        first, count = own - reach, rows + 2 * reach
        if count >= X:
            first, count = 0, X
            flux_rows(make, 0, X, True)
            for ref in (fx, vis):
                ref[:, :REACH] = ref[:, X : X + REACH]
                ref[:, X + REACH :] = ref[:, REACH : 2 * REACH]
        else:
            flux_rows(make, first, count, True)
            flux_rows(make, first - REACH, REACH, False)
            flux_rows(make, first + count, REACH, False)
        if last:
            stencil_rows(target, first, first, count, side * half, half)
        else:
            stencil_rows(target, first, first, count, 0, Y)

    def rows_of(ref, f, x, n):
        return ref[f, pl.ds(x - (X - ref.shape[1]) // 2, n)]

    def mix(*terms):
        def make(f, x, n):
            total = None
            for weight, ref in terms:
                value = rows_of(ref, f, x, n)
                value = value if weight == 1 else weight * value
                total = value if total is None else total + value
            return total

        return make

    half_step, five, sixth, twelfth = 0.5, 5.0 / 12.0, 1.0 / 6.0, 1.0 / 12.0
    u01 = mix((1, base), (1, G0))
    u02 = mix((1, base), (1, G0), (1, A1))
    u03 = mix((1, base), (1, G0), (1, A1), (1, A2))
    u11 = mix((1, base), (half_step, G0), (half_step, A1))
    u12 = mix((1, base), (five, G0), (sixth, A1), (1, B1), (five, A2))
    u13 = mix((1, base), (five, G0), (twelfth, A1), (1, B1), (twelfth, A2), (1, B2), (five, A3))
    u21 = mix((1, base), (half_step, G0), (half_step, B1))
    u22 = mix((1, base), (five, G0), (sixth, B1), (1, C1), (five, B2))
    u23 = mix((1, base), (five, G0), (twelfth, B1), (1, C1), (twelfth, B2), (1, C2), (five, B3))
    u31 = mix((1, base), (half_step, G0), (half_step, C1))
    u32 = mix((1, base), (five, G0), (sixth, C1), (1, D1), (five, C2))
    u33 = mix((1, base), (five, G0), (twelfth, C1), (1, D1), (twelfth, C2), (1, D2), (five, C3))

    tendency(G0, mix((1, base)), 5 * REACH)
    tendency(A1, u01, 4 * REACH)
    tendency(A2, u02, 3 * REACH)
    tendency(B1, u11, 3 * REACH)
    tendency(A3, u03, 2 * REACH)
    tendency(B2, u12, 2 * REACH)
    tendency(C1, u21, 2 * REACH)
    tendency(B3, u13, REACH)
    tendency(C2, u22, REACH)
    tendency(D1, u31, REACH)
    tendency(C3, u23, 0, last=True)
    tendency(D2, u32, 0, last=True)

    at = pl.multiple_of(side * half, half)
    for p, terms in enumerate(
        (
            ((1, base), (1, G0), (1, A1), (1, A2)),
            ((1, base), (five, G0), (twelfth, A1), (1, B1), (twelfth, A2), (1, B2), (five, A3)),
            ((1, base), (five, G0), (twelfth, B1), (1, C1), (twelfth, B2), (1, C2), (five, B3)),
            ((1, base), (five, G0), (twelfth, C1), (1, D1), (twelfth, C2), (1, D2), (five, C3)),
        )
    ):

        @pl.when(level == p)
        def _():
            for f in range(fields):
                total = None
                for weight, ref in terms:
                    start = own - (X - ref.shape[1]) // 2
                    value = ref[f, start : start + rows, pl.ds(at, half), :]
                    value = value if weight == 1 else weight * value
                    total = value if total is None else total + value
                out[0, f] = total


def run_levels(where, mine, theirs, gx):
    fields, rows, half, Z = mine[0].shape
    X, Y = rows * gx, 2 * half
    first_z, second_z = circulants(Z)
    first_y, second_y = circulants(Y)
    bf16 = ml_dtypes.bfloat16
    wz_first = np.concatenate([first_z.T, first_z.T], axis=0).astype(bf16)
    wz_second = np.concatenate([second_z.T, second_z.T], axis=0).astype(bf16)
    wy = np.concatenate([first_y, first_y, second_y, second_y], axis=1).astype(bf16)

    def hold(n, lead=fields):
        return pltpu.VMEM((lead, n, Y, Z), jnp.float32)

    scratch = [hold(X), hold(X + 2 * REACH), hold(X + 2 * REACH, fields - 1), hold(X)]
    for reach in (5, 4, 3, 3, 2, 2, 2, 1, 1, 1, 0, 0):
        scratch.append(hold(min(X, rows + 2 * reach * REACH)))
    vmem = pl.BlockSpec(memory_space=pltpu.VMEM)
    return pl.pallas_call(
        functools.partial(levels_kernel, rows),
        out_shape=jax.ShapeDtypeStruct((1, fields, rows, half, Z), jnp.float32),
        in_specs=[pl.BlockSpec(memory_space=pltpu.SMEM)] + [vmem] * (2 * gx + 3),
        out_specs=vmem,
        scratch_shapes=scratch,
        compiler_params=pltpu.CompilerParams(vmem_limit_bytes=VMEM_BUDGET),
    )(where, *mine, *theirs, wz_first, wz_second, wy)


def gathered_body(state):
    gx = lax.axis_size("gx")
    where = jnp.stack([lax.axis_index("level"), lax.axis_index("gy")]).astype(jnp.int32)
    mine = [state]
    for ahead in range(1, gx):
        route = [((i + ahead) % gx, i) for i in range(gx)]
        mine.append(lax.ppermute(state, "gx", route))
    theirs = [lax.ppermute(piece, "gy", [(0, 1), (1, 0)]) for piece in mine]
    return run_levels(where, mine, theirs, gx)


def with_halo(block, sides, width):
    for axis, dim in sides:
        count = lax.axis_size(axis)
        forward = [(i, i + 1) for i in range(count - 1)]
        forward.append((count - 1, 0))
        backward = [(target, source) for source, target in forward]
        low = lax.ppermute(
            lax.slice_in_dim(block, block.shape[dim] - width, None, axis=dim), axis, forward
        )
        high = lax.ppermute(lax.slice_in_dim(block, 0, width, axis=dim), axis, backward)
        block = jnp.concatenate([low, block, high], axis=dim)
    return block


def shifted_2(block, axis, distance):
    devices = range(lax.axis_size(axis))
    route = [(i - distance, i) for i in devices if i - distance in devices]
    return lax.ppermute(block, axis, route)


def shifted(quantity, direction, offset):
    extent = quantity.shape[-3:]
    picks = [slice(4, extent[0] - 4), slice(4, extent[1] - 4), slice(4, extent[2] - 4)]
    picks[direction] = slice(4 + offset, extent[direction] - 4 + offset)
    leading = (slice(None),) * (quantity.ndim - 3)
    return quantity[leading + tuple(picks)]


def first_derivative(quantity, direction):
    total = 0.0
    for position, weight in enumerate(FIRST_COEF):
        total = total + weight * (
            shifted(quantity, direction, position + 1) - shifted(quantity, direction, -position - 1)
        )
    return total


def second_derivative_sum(quantity):
    total = 0.0
    for direction in range(3):
        total = total + SECOND_CENTER * shifted(quantity, direction, 0)
        for position, weight in enumerate(SECOND_COEF):
            total = total + weight * (
                shifted(quantity, direction, position + 1)
                + shifted(quantity, direction, -position - 1)
            )
    return total


def tendency(padded):
    specific_volume_inverse = padded[0]
    momentum = padded[1:4]
    energy = padded[4]
    velocity = momentum / specific_volume_inverse
    kinetic_energy_share = 0.5 * jnp.sum(velocity * velocity, axis=0)
    normal_stress_scalar = (GAMMA - 1.0) * (energy - specific_volume_inverse * kinetic_energy_share)
    absolute_kelvin_value = normal_stress_scalar / specific_volume_inverse
    divergence = 0.0
    for direction in range(3):
        along = velocity[direction]
        rows = [
            momentum[component] * along + (normal_stress_scalar if component == direction else 0.0)
            for component in range(3)
        ]
        flux = jnp.stack([momentum[direction]] + rows + [(energy + normal_stress_scalar) * along])
        divergence = divergence + first_derivative(flux, direction)
    viscous = SHEAR_COEFFICIENT * second_derivative_sum(velocity)
    conduction_contribution = SHEAR_COEFFICIENT * second_derivative_sum(
        kinetic_energy_share
    ) + CONDUCTIVITY * second_derivative_sum(absolute_kelvin_value)
    return jnp.concatenate(
        [
            -divergence[0:1],
            viscous - divergence[1:4],
            (conduction_contribution - divergence[4])[None],
        ],
        axis=0,
    )


def wrap_depth(field):
    return jnp.concatenate([field[:, :, :, -4:], field, field[:, :, :, :4]], axis=3)


def padded_faces(field):
    return wrap_depth(with_halo(field, (("gx", 1), ("gy", 2)), 4))


def sections_body(state):
    levels = lax.axis_size("level")
    rank = lax.axis_index("level")
    current = state
    before = jnp.zeros_like(state)
    middle = jnp.zeros_like(state)
    for section in range(STEPS + levels - 1):
        node = section - rank
        forcing = tendency(padded_faces(current))
        newest = shifted_2(forcing, "level", 1)
        quad_term = jnp.where(
            node == 0, 0.5 * (middle + newest), (8.0 * middle + 5.0 * newest - before) / 12.0
        )
        moved = current + DT * (forcing - middle + quad_term)
        active = jnp.logical_and(node >= 0, node < STEPS)
        current = jnp.where(active, moved, current)
        before = middle
        middle = newest
    return current[None]


def body(state):
    fields, rows, half, Z = state.shape
    gx, gy, levels = lax.axis_size("gx"), lax.axis_size("gy"), lax.axis_size("level")
    X, Y = rows * gx, half * gy
    need = 4 * fields * Y * Z * 15 * X
    simple = gy == 2 and levels == 4 and Z == 128 and Y % 32 == 0 and rows == 2 * REACH and half % 16 == 0
    if simple and gx % 2 == 0 and X <= rows + 6 * REACH and need <= VMEM_BUDGET:
        return gathered_body(state)
    return sections_body(state)


def solution(mesh):
    return jax.shard_map(
        body,
        mesh=mesh,
        in_specs=(P(None, "gx", "gy", None),),
        out_specs=P("level", None, "gx", "gy", None),
        check_vma=False,
    )
```

```python
import functools

import jax
import jax.numpy as jnp
import ml_dtypes
import numpy as np
from jax import lax
from jax.experimental import pallas as pl
from jax.experimental.pallas import tpu as pltpu
from jax.sharding import PartitionSpec as P

STEPS = 3


DT = 0.1
GAMMA = 1.4
SHEAR_COEFFICIENT = 0.1
CONDUCTIVITY = 0.1
FIRST_COEF = (4.0 / 5.0, -1.0 / 5.0, 4.0 / 105.0, -1.0 / 280.0)
SECOND_CENTER = -205.0 / 72.0
SECOND_COEF = (8.0 / 5.0, -1.0 / 5.0, 8.0 / 315.0, -1.0 / 560.0)
REACH = 4
SCALE = 5040
FIRST_WHOLE = tuple(round(w * SCALE) for w in FIRST_COEF)
SECOND_WHOLE = tuple(round(w * SCALE) for w in SECOND_COEF)
VMEM_BUDGET = 56 * 1024 * 1024
FLUX_ROWS = 8
MIDDLE = 0.07


def circulants(extent):
    first = np.zeros((extent, extent), np.float32)
    second = np.zeros((extent, extent), np.float32)
    for place in range(extent):
        for k in range(1, REACH + 1):
            first[place, (place + k) % extent] -= FIRST_WHOLE[k - 1]
            first[place, (place - k) % extent] += FIRST_WHOLE[k - 1]
            second[place, (place + k) % extent] += SECOND_WHOLE[k - 1]
            second[place, (place - k) % extent] += SECOND_WHOLE[k - 1]
    return first, second


def split(value):
    high = value.astype(jnp.bfloat16)
    low = (value - high.astype(jnp.float32)).astype(jnp.bfloat16)
    return high, low


def levels_kernel(rows, n_near, n_far, where, *refs):
    near, far = refs[:n_near], refs[n_near : n_near + n_far]
    refs = refs[n_near + n_far :]
    wz_first, wz_second, wy, wxy, out = refs[:5]
    base, *held = refs[5:]
    fx, vis, part, G0, A1, A2, B1, A3, B2, C1, B3, C2, D1, C3, D2 = held
    fields, X, Y, Z = base.shape
    half = near[0].shape[2]
    level, side = where[0], where[1]
    own = (X - rows) // 2

    quarter = rows // 4

    def lay(value, core, ahead, e):
        at = pl.multiple_of(core * half, half)
        x = own + ahead * rows
        if e is None:
            base[:, x : x + rows, pl.ds(at, half), :] = value
        else:
            x = x + quarter * (level ^ e)
            x = jnp.where(x >= X, x - X, x)
            base[:, pl.ds(x, quarter), pl.ds(at, half), :] = value

    lay(near[0][...], side, 0, None)
    lay(far[0][...], 1 - side, 0, None)
    for ahead in range(1, X // rows):
        for e in range(4):
            lay(near[4 * ahead - 3 + e][...], side, ahead, e)
            lay(far[ahead][e], 1 - side, ahead, e)

    def pointwise(u):
        rho, m0, m1, m2, energy = u
        inverse = 1.0 / rho
        v0, v1, v2 = m0 * inverse, m1 * inverse, m2 * inverse
        m00, m11, m22 = m0 * v0, m1 * v1, m2 * v2
        m01, m02, m12 = m0 * v1, m0 * v2, m1 * v2
        twice = m00 + m11 + m22
        p = (GAMMA - 1.0) * energy - (0.5 * (GAMMA - 1.0)) * twice
        heat = energy + p
        warm = inverse * ((0.5 * SHEAR_COEFFICIENT) * twice + CONDUCTIVITY * p) - MIDDLE
        s = SHEAR_COEFFICIENT
        g = [s * v0, s * v1, s * v2, warm]
        along_x = [m0, m00 + p, m01, m02, heat * v0]
        along_y = [m1, m01, m11 + p, m12, heat * v1]
        along_z = [m2, m02, m12, m22 + p, heat * v2]
        return along_x, along_y, along_z, g

    def flux_rows(make, first, count, whole):
        batch = min(FLUX_ROWS, count)

        def step(i, carry):
            x = first + i * batch
            u = [make(f, x, batch).reshape(batch * Y, Z) for f in range(fields)]
            along_x, along_y, along_z, g = pointwise(u)
            for f in range(fields):
                fx[f, pl.ds(x + REACH, batch)] = along_x[f].reshape(batch, Y, Z)
            g = jnp.concatenate([v.astype(jnp.bfloat16) for v in g], axis=1)
            vis[pl.ds(pl.multiple_of((x + REACH) * Y, Y), batch * Y), :] = g
            if whole:
                zs = [split(v) for v in along_z]
                ys = [split(v) for v in along_y]
                flux = jnp.concatenate([jnp.concatenate(pair, axis=1) for pair in zs], axis=0)
                flux = jnp.dot(flux, wz_first[...], preferred_element_type=jnp.float32)
                soft = jnp.concatenate([g[:, : 2 * Z], g[:, 2 * Z :]], axis=0)
                soft = jnp.dot(soft, wz_second[...], preferred_element_type=jnp.float32)
                group = wy.shape[0] // Y
                for r in range(0, batch, group):
                    columns = []
                    for f in range(fields):
                        cuts = [slice((r + q) * Y, (r + q + 1) * Y) for q in range(group)]
                        columns.append(jnp.concatenate([v[cut] for cut in cuts for v in ys[f]], axis=0))
                    deep = jnp.dot(wy[...], jnp.concatenate(columns, axis=1), preferred_element_type=jnp.float32)
                    for f in range(fields):
                        at = f * batch * Y + r * Y
                        total = deep[:, f * Z : (f + 1) * Z] + flux[at : at + group * Y]
                        if f:
                            at = ((f - 1) // 2) * batch * Y + r * Y
                            lane = ((f - 1) % 2) * Z
                            total = total + soft[at : at + group * Y, lane : lane + Z]
                        part[f, pl.ds(x + r, group)] = total.reshape(group, Y, Z)
            return carry

        lax.fori_loop(0, count // batch, step, 0)

    def stencil_rows(target, shift, first, count):
        block = wxy.shape[0] // Y

        def soften(x):
            g = [vis[x * Y : (x + block + 2 * REACH) * Y, 2 * p * Z : 2 * (p + 1) * Z] for p in range(2)]
            return [jnp.dot(wxy[...], v, preferred_element_type=jnp.float32).reshape(block, Y, 2 * Z) for v in g]

        def end(x, soft):
            for f in range(fields):
                for y in range(0, Y, 8):
                    flux = fx[f, x : x + block + 2 * REACH, y : y + 8, :]
                    total = part[f, x : x + block, y : y + 8, :]
                    if f:
                        pair, place = divmod(f - 1, 2)
                        total = total + soft[pair][:, y : y + 8, place * Z : (place + 1) * Z]
                    for k in range(1, REACH + 1):
                        ahead = slice(REACH + k, REACH + k + block)
                        behind = slice(REACH - k, REACH - k + block)
                        total = total + float(FIRST_WHOLE[k - 1]) * (flux[behind] - flux[ahead])
                    target[f, x - shift : x - shift + block, y : y + 8, :] = (DT / SCALE) * total

        places = range(first, first + count, block)
        soft = soften(places[0])
        for x in places:
            following = soften(x + block) if x + block < first + count else None
            end(x, soft)
            soft = following

    def tendency(target, make, reach):
        first, count = own - reach, rows + 2 * reach
        if count >= X:
            first, count = 0, X
            flux_rows(make, 0, X, True)
            edge = REACH * Y
            fx[:, :REACH] = fx[:, X : X + REACH]
            fx[:, X + REACH :] = fx[:, REACH : 2 * REACH]
            vis[:edge] = vis[X * Y : X * Y + edge]
            vis[X * Y + edge :] = vis[edge : 2 * edge]
        else:
            flux_rows(make, first, count, True)
            flux_rows(make, first - REACH, REACH, False)
            flux_rows(make, first + count, REACH, False)
        stencil_rows(target, first, first, count)

    def rows_of(ref, f, x, n):
        return ref[f, pl.ds(x - (X - ref.shape[1]) // 2, n)]

    half_step, five, sixth, twelfth = 0.5, 5.0 / 12.0, 1.0 / 6.0, 1.0 / 12.0

    def mix(*terms):
        def make(f, x, n):
            total = None
            for weight, *held in terms:
                value = rows_of(held[0], f, x, n)
                for ref in held[1:]:
                    value = value + rows_of(ref, f, x, n)
                value = value if weight == 1 else weight * value
                total = value if total is None else total + value
            return total

        return make

    def second(g, low, mid, high):
        return mix((1, base, mid), (five, g, high), (sixth, low))

    u03 = ((1, base, G0, A1, A2),)
    u13 = ((1, base, B1, B2), (five, G0, A3), (twelfth, A1, A2))
    u23 = ((1, base, C1, C2), (five, G0, B3), (twelfth, B1, B2))
    u33 = ((1, base, D1, D2), (five, G0, C3), (twelfth, C1, C2))

    tendency(G0, mix((1, base)), 5 * REACH)
    tendency(A1, mix((1, base, G0)), 4 * REACH)
    tendency(A2, mix((1, base, G0, A1)), 3 * REACH)
    tendency(B1, mix((1, base), (half_step, G0, A1)), 3 * REACH)
    tendency(A3, mix(*u03), 2 * REACH)
    tendency(B2, second(G0, A1, B1, A2), 2 * REACH)
    tendency(C1, mix((1, base), (half_step, G0, B1)), 2 * REACH)
    tendency(B3, mix(*u13), REACH)
    tendency(C2, second(G0, B1, C1, B2), REACH)
    tendency(D1, mix((1, base), (half_step, G0, C1)), REACH)
    tendency(C3, mix(*u23), 0)
    tendency(D2, second(G0, C1, D1, C2), 0)

    at = pl.multiple_of(side * half, half)
    for p, terms in enumerate((u03, u13, u23, u33)):

        @pl.when(level == p)
        def _():
            for f in range(fields):
                total = None
                for weight, *held in terms:
                    value = None
                    for ref in held:
                        start = own - (X - ref.shape[1]) // 2
                        here = ref[f, start : start + rows, pl.ds(at, half), :]
                        value = here if value is None else value + here
                    value = value if weight == 1 else weight * value
                    total = value if total is None else total + value
                out[0, f] = total


def run_levels(where, near, far, gx):
    fields, rows, half, Z = near[0].shape
    X, Y = rows * gx, 2 * half
    bf16 = ml_dtypes.bfloat16
    first_z, second_z = circulants(Z)
    first_y, second_y = circulants(Y)
    centre = round(3 * SECOND_CENTER * SCALE)
    coarse = int(np.float32(bf16(centre)))
    second_z = second_z + (centre - coarse) * np.eye(Z, dtype=np.float32)
    second_y = second_y + coarse * np.eye(Y, dtype=np.float32)
    wz_first = np.concatenate([first_z.T, first_z.T], axis=0).astype(bf16)
    wz_second = np.kron(np.eye(2, dtype=np.float32), second_z.T).astype(bf16)
    group = max(1, 128 // Y)
    wy = np.kron(np.eye(group, dtype=np.float32), np.concatenate([first_y, first_y], axis=1)).astype(bf16)
    block = rows
    wxy = np.zeros((block, Y, block + 2 * REACH, Y), np.float32)
    for x in range(block):
        wxy[x, :, x + REACH, :] = second_y
        for k in range(1, REACH + 1):
            wxy[x, :, x + REACH + k, :] = SECOND_WHOLE[k - 1] * np.eye(Y, dtype=np.float32)
            wxy[x, :, x + REACH - k, :] = SECOND_WHOLE[k - 1] * np.eye(Y, dtype=np.float32)
    wxy = wxy.reshape(block * Y, (block + 2 * REACH) * Y).astype(bf16)

    def hold(n):
        return pltpu.VMEM((fields, n, Y, Z), jnp.float32)

    soft = pltpu.VMEM(((X + 2 * REACH) * Y, (fields - 1) * Z), jnp.bfloat16)
    scratch = [hold(X), hold(X + 2 * REACH), soft, hold(X)]
    for reach in (5, 4, 3, 3, 2, 2, 2, 1, 1, 1, 0, 0):
        scratch.append(hold(min(X, rows + 2 * reach * REACH)))
    vmem = pl.BlockSpec(memory_space=pltpu.VMEM)
    return pl.pallas_call(
        functools.partial(levels_kernel, rows, len(near), len(far)),
        out_shape=jax.ShapeDtypeStruct((1, fields, rows, half, Z), jnp.float32),
        in_specs=[pl.BlockSpec(memory_space=pltpu.SMEM)] + [vmem] * (len(near) + len(far) + 4),
        out_specs=vmem,
        scratch_shapes=scratch,
        compiler_params=pltpu.CompilerParams(vmem_limit_bytes=VMEM_BUDGET),
    )(where, *near, *far, wz_first, wz_second, wy, wxy)


def gathered_body(state):
    gx, levels = lax.axis_size("gx"), lax.axis_size("level")
    level = lax.axis_index("level")
    where = jnp.stack([level, lax.axis_index("gy")]).astype(jnp.int32)
    swap = [(0, 1), (1, 0)]
    quarter = state.shape[1] // levels
    mine = lax.dynamic_slice_in_dim(state, level * quarter, quarter, axis=1)
    near, far = [state], [lax.ppermute(state, "gy", swap)]
    for ahead in range(1, gx):
        route = [((i + ahead) % gx, i) for i in range(gx)]
        first = lax.ppermute(mine, "gx", route)
        parts = [first]
        for e in range(1, levels):
            parts.append(lax.ppermute(first, "level", [(i, i ^ e) for i in range(levels)]))
        near += parts
        far.append(lax.ppermute(jnp.stack(parts), "gy", swap))
    return run_levels(where, near, far, gx)


def with_halo(block, sides, width):
    for axis, dim in sides:
        count = lax.axis_size(axis)
        forward = [(i, i + 1) for i in range(count - 1)]
        forward.append((count - 1, 0))
        backward = [(target, source) for source, target in forward]
        low = lax.ppermute(
            lax.slice_in_dim(block, block.shape[dim] - width, None, axis=dim), axis, forward
        )
        high = lax.ppermute(lax.slice_in_dim(block, 0, width, axis=dim), axis, backward)
        block = jnp.concatenate([low, block, high], axis=dim)
    return block


def shifted_2(block, axis, distance):
    devices = range(lax.axis_size(axis))
    route = [(i - distance, i) for i in devices if i - distance in devices]
    return lax.ppermute(block, axis, route)


def shifted(quantity, direction, offset):
    extent = quantity.shape[-3:]
    picks = [slice(4, extent[0] - 4), slice(4, extent[1] - 4), slice(4, extent[2] - 4)]
    picks[direction] = slice(4 + offset, extent[direction] - 4 + offset)
    leading = (slice(None),) * (quantity.ndim - 3)
    return quantity[leading + tuple(picks)]


def first_derivative(quantity, direction):
    total = 0.0
    for position, weight in enumerate(FIRST_COEF):
        total = total + weight * (
            shifted(quantity, direction, position + 1) - shifted(quantity, direction, -position - 1)
        )
    return total


def second_derivative_sum(quantity):
    total = 0.0
    for direction in range(3):
        total = total + SECOND_CENTER * shifted(quantity, direction, 0)
        for position, weight in enumerate(SECOND_COEF):
            total = total + weight * (
                shifted(quantity, direction, position + 1)
                + shifted(quantity, direction, -position - 1)
            )
    return total


def tendency(padded):
    specific_volume_inverse = padded[0]
    momentum = padded[1:4]
    energy = padded[4]
    velocity = momentum / specific_volume_inverse
    kinetic_energy_share = 0.5 * jnp.sum(velocity * velocity, axis=0)
    normal_stress_scalar = (GAMMA - 1.0) * (energy - specific_volume_inverse * kinetic_energy_share)
    absolute_kelvin_value = normal_stress_scalar / specific_volume_inverse
    divergence = 0.0
    for direction in range(3):
        along = velocity[direction]
        rows = [
            momentum[component] * along + (normal_stress_scalar if component == direction else 0.0)
            for component in range(3)
        ]
        flux = jnp.stack([momentum[direction]] + rows + [(energy + normal_stress_scalar) * along])
        divergence = divergence + first_derivative(flux, direction)
    viscous = SHEAR_COEFFICIENT * second_derivative_sum(velocity)
    conduction_contribution = SHEAR_COEFFICIENT * second_derivative_sum(
        kinetic_energy_share
    ) + CONDUCTIVITY * second_derivative_sum(absolute_kelvin_value)
    return jnp.concatenate(
        [
            -divergence[0:1],
            viscous - divergence[1:4],
            (conduction_contribution - divergence[4])[None],
        ],
        axis=0,
    )


def wrap_depth(field):
    return jnp.concatenate([field[:, :, :, -4:], field, field[:, :, :, :4]], axis=3)


def padded_faces(field):
    return wrap_depth(with_halo(field, (("gx", 1), ("gy", 2)), 4))


def sections_body(state):
    levels = lax.axis_size("level")
    rank = lax.axis_index("level")
    current = state
    before = jnp.zeros_like(state)
    middle = jnp.zeros_like(state)
    for section in range(STEPS + levels - 1):
        node = section - rank
        forcing = tendency(padded_faces(current))
        newest = shifted_2(forcing, "level", 1)
        quad_term = jnp.where(
            node == 0, 0.5 * (middle + newest), (8.0 * middle + 5.0 * newest - before) / 12.0
        )
        moved = current + DT * (forcing - middle + quad_term)
        active = jnp.logical_and(node >= 0, node < STEPS)
        current = jnp.where(active, moved, current)
        before = middle
        middle = newest
    return current[None]


def body(state):
    fields, rows, half, Z = state.shape
    gx, gy, levels = lax.axis_size("gx"), lax.axis_size("gy"), lax.axis_size("level")
    X, Y = rows * gx, half * gy
    need = 4 * fields * Y * Z * 15 * X
    simple = gy == 2 and levels == 4 and Z == 128 and Y % 32 == 0 and rows == 2 * REACH and rows % levels == 0 and half % 16 == 0
    if simple and gx % 2 == 0 and X <= rows + 6 * REACH and need <= VMEM_BUDGET:
        return gathered_body(state)
    return sections_body(state)


def solution(mesh):
    return jax.shard_map(
        body,
        mesh=mesh,
        in_specs=(P(None, "gx", "gy", None),),
        out_specs=P("level", None, "gx", "gy", None),
        check_vma=False,
    )
```

```python
import functools

import jax
import jax.numpy as jnp
import ml_dtypes
import numpy as np
from jax import lax
from jax.experimental import pallas as pl
from jax.experimental.pallas import tpu as pltpu
from jax.sharding import PartitionSpec as P

STEPS = 3


DT = 0.1
GAMMA = 1.4
SHEAR_COEFFICIENT = 0.1
CONDUCTIVITY = 0.1
FIRST_COEF = (4.0 / 5.0, -1.0 / 5.0, 4.0 / 105.0, -1.0 / 280.0)
SECOND_CENTER = -205.0 / 72.0
SECOND_COEF = (8.0 / 5.0, -1.0 / 5.0, 8.0 / 315.0, -1.0 / 560.0)
REACH = 4
SCALE = 5040
FIRST_WHOLE = tuple(round(w * SCALE) for w in FIRST_COEF)
SECOND_WHOLE = tuple(round(w * SCALE) for w in SECOND_COEF)
VMEM_BUDGET = 56 * 1024 * 1024
FLUX_ROWS = 8
MIDDLE = 0.07


def circulants(extent):
    first = np.zeros((extent, extent), np.float32)
    second = np.zeros((extent, extent), np.float32)
    for place in range(extent):
        for k in range(1, REACH + 1):
            first[place, (place + k) % extent] -= FIRST_WHOLE[k - 1]
            first[place, (place - k) % extent] += FIRST_WHOLE[k - 1]
            second[place, (place + k) % extent] += SECOND_WHOLE[k - 1]
            second[place, (place - k) % extent] += SECOND_WHOLE[k - 1]
    return first, second


def split(value):
    high = value.astype(jnp.bfloat16)
    low = (value - high.astype(jnp.float32)).astype(jnp.bfloat16)
    return high, low


def levels_kernel(rows, n_near, n_far, *refs):
    near, far = refs[:n_near], refs[n_near : n_near + n_far]
    refs = refs[n_near + n_far :]
    wz_first, wz_second, wy, wxy, out = refs[:5]
    base, *held = refs[5:]
    fx, vis, part, G0, A1, A2, B1, A3, B2, C1, B3, C2, D1, C3, D2 = held
    fields, X, Y, Z = base.shape
    half = near[0].shape[2]
    level, side = lax.axis_index("level"), lax.axis_index("gy")
    own = (X - rows) // 2

    quarter = rows // 4

    def lay(value, core, ahead, e):
        at = pl.multiple_of(core * half, half)
        x = own + ahead * rows
        if e is None:
            base[:, x : x + rows, pl.ds(at, half), :] = value
        else:
            x = x + quarter * (level ^ e)
            x = jnp.where(x >= X, x - X, x)
            base[:, pl.ds(x, quarter), pl.ds(at, half), :] = value

    lay(near[0][...], side, 0, None)
    lay(far[0][...], 1 - side, 0, None)
    for ahead in range(1, X // rows):
        for e in range(4):
            lay(near[4 * ahead - 3 + e][...], side, ahead, e)
            lay(far[ahead][e], 1 - side, ahead, e)

    def pointwise(u):
        rho, m0, m1, m2, energy = u
        inverse = 1.0 / rho
        v0, v1, v2 = m0 * inverse, m1 * inverse, m2 * inverse
        m00, m11, m22 = m0 * v0, m1 * v1, m2 * v2
        m01, m02, m12 = m0 * v1, m0 * v2, m1 * v2
        twice = m00 + m11 + m22
        p = (GAMMA - 1.0) * energy - (0.5 * (GAMMA - 1.0)) * twice
        heat = energy + p
        warm = inverse * ((0.5 * SHEAR_COEFFICIENT) * twice + CONDUCTIVITY * p) - MIDDLE
        s = SHEAR_COEFFICIENT
        g = [s * v0, s * v1, s * v2, warm]
        along_x = [m0, m00 + p, m01, m02, heat * v0]
        along_y = [m1, m01, m11 + p, m12, heat * v1]
        along_z = [m2, m02, m12, m22 + p, heat * v2]
        return along_x, along_y, along_z, g

    def flux_rows(make, first, count, whole):
        batch = min(FLUX_ROWS, count)

        def produce(x):
            u = [make(f, x, batch).reshape(batch * Y, Z) for f in range(fields)]
            along_x, along_y, along_z, g = pointwise(u)
            for f in range(fields):
                fx[f, pl.ds(x + REACH, batch)] = along_x[f].reshape(batch, Y, Z)
            g = jnp.concatenate([v.astype(jnp.bfloat16) for v in g], axis=1)
            at = (x + REACH) * Y
            vis[pl.ds(at if isinstance(at, int) else pl.multiple_of(at, Y), batch * Y), :] = g
            if whole:
                zs = [split(v) for v in along_z]
                ys = [split(v) for v in along_y]
                flux = jnp.concatenate([jnp.concatenate(pair, axis=1) for pair in zs], axis=0)
                flux = jnp.dot(flux, wz_first[...], preferred_element_type=jnp.float32)
                soft = jnp.concatenate([g[:, : 2 * Z], g[:, 2 * Z :]], axis=0)
                soft = jnp.dot(soft, wz_second[...], preferred_element_type=jnp.float32)
                group = wy.shape[0] // Y
                deeps = []
                for r in range(0, batch, group):
                    columns = []
                    for f in range(fields):
                        cuts = [slice((r + q) * Y, (r + q + 1) * Y) for q in range(group)]
                        columns.append(jnp.concatenate([v[cut] for cut in cuts for v in ys[f]], axis=0))
                    columns = jnp.concatenate(columns, axis=1)
                    deeps.append(jnp.dot(wy[...], columns, preferred_element_type=jnp.float32))
                return flux, soft, deeps
            return None

        def keep(x, flux, soft, deeps):
            group = wy.shape[0] // Y
            for r in range(0, batch, group):
                deep = deeps[r // group]
                for f in range(fields):
                    at = f * batch * Y + r * Y
                    total = deep[:, f * Z : (f + 1) * Z] + flux[at : at + group * Y]
                    if f:
                        at = ((f - 1) // 2) * batch * Y + r * Y
                        lane = ((f - 1) % 2) * Z
                        total = total + soft[at : at + group * Y, lane : lane + Z]
                    part[f, pl.ds(x + r, group)] = total.reshape(group, Y, Z)

        def step(i, carry):
            made = [(x, produce(x)) for x in (first + i * count + j for j in range(0, count, batch))]
            for x, values in made:
                if values:
                    keep(x, *values)
            return carry

        lax.fori_loop(0, 1, step, 0)

    def stencil_rows(target, shift, first, count):
        block = wxy.shape[0] // Y

        def soften(x):
            g = [vis[x * Y : (x + block + 2 * REACH) * Y, 2 * p * Z : 2 * (p + 1) * Z] for p in range(2)]
            return [jnp.dot(wxy[...], v, preferred_element_type=jnp.float32).reshape(block, Y, 2 * Z) for v in g]

        def end(x, soft):
            for f in range(fields):
                for y in range(0, Y, 8):
                    flux = fx[f, x : x + block + 2 * REACH, y : y + 8, :]
                    total = part[f, x : x + block, y : y + 8, :]
                    if f:
                        pair, place = divmod(f - 1, 2)
                        total = total + soft[pair][:, y : y + 8, place * Z : (place + 1) * Z]
                    for k in range(1, REACH + 1):
                        ahead = slice(REACH + k, REACH + k + block)
                        behind = slice(REACH - k, REACH - k + block)
                        total = total + float(FIRST_WHOLE[k - 1]) * (flux[behind] - flux[ahead])
                    target[f, x - shift : x - shift + block, y : y + 8, :] = (DT / SCALE) * total

        places = range(first, first + count, block)
        soft = soften(places[0])
        for x in places:
            following = soften(x + block) if x + block < first + count else None
            end(x, soft)
            soft = following

    def tendency(target, make, reach):
        first, count = own - reach, rows + 2 * reach
        if count >= X:
            first, count = 0, X
            flux_rows(make, 0, X, True)
            edge = REACH * Y
            fx[:, :REACH] = fx[:, X : X + REACH]
            fx[:, X + REACH :] = fx[:, REACH : 2 * REACH]
            vis[:edge] = vis[X * Y : X * Y + edge]
            vis[X * Y + edge :] = vis[edge : 2 * edge]
        else:
            flux_rows(make, first, count, True)
            flux_rows(make, first - REACH, REACH, False)
            flux_rows(make, first + count, REACH, False)
        stencil_rows(target, first, first, count)

    def rows_of(ref, f, x, n):
        return ref[f, pl.ds(x - (X - ref.shape[1]) // 2, n)]

    half_step, five, sixth, twelfth = 0.5, 5.0 / 12.0, 1.0 / 6.0, 1.0 / 12.0

    def mix(*terms):
        def make(f, x, n):
            total = None
            for weight, *held in terms:
                value = rows_of(held[0], f, x, n)
                for ref in held[1:]:
                    value = value + rows_of(ref, f, x, n)
                value = value if weight == 1 else weight * value
                total = value if total is None else total + value
            return total

        return make

    def second(g, low, mid, high):
        return mix((1, base, mid), (five, g, high), (sixth, low))

    u03 = ((1, base, G0, A1, A2),)
    u13 = ((1, base, B1, B2), (five, G0, A3), (twelfth, A1, A2))
    u23 = ((1, base, C1, C2), (five, G0, B3), (twelfth, B1, B2))
    u33 = ((1, base, D1, D2), (five, G0, C3), (twelfth, C1, C2))

    tendency(G0, mix((1, base)), 5 * REACH)
    tendency(A1, mix((1, base, G0)), 4 * REACH)
    tendency(A2, mix((1, base, G0, A1)), 3 * REACH)
    tendency(B1, mix((1, base), (half_step, G0, A1)), 3 * REACH)
    tendency(A3, mix(*u03), 2 * REACH)
    tendency(B2, second(G0, A1, B1, A2), 2 * REACH)
    tendency(C1, mix((1, base), (half_step, G0, B1)), 2 * REACH)
    tendency(B3, mix(*u13), REACH)
    tendency(C2, second(G0, B1, C1, B2), REACH)
    tendency(D1, mix((1, base), (half_step, G0, C1)), REACH)
    tendency(C3, mix(*u23), 0)
    tendency(D2, second(G0, C1, D1, C2), 0)

    at = pl.multiple_of(side * half, half)
    for p, terms in enumerate((u03, u13, u23, u33)):

        @pl.when(level == p)
        def _():
            for f in range(fields):
                total = None
                for weight, *held in terms:
                    value = None
                    for ref in held:
                        start = own - (X - ref.shape[1]) // 2
                        here = ref[f, start : start + rows, pl.ds(at, half), :]
                        value = here if value is None else value + here
                    value = value if weight == 1 else weight * value
                    total = value if total is None else total + value
                out[0, f] = total


def run_levels(near, far, gx):
    fields, rows, half, Z = near[0].shape
    X, Y = rows * gx, 2 * half
    bf16 = ml_dtypes.bfloat16
    first_z, second_z = circulants(Z)
    first_y, second_y = circulants(Y)
    centre = round(3 * SECOND_CENTER * SCALE)
    coarse = int(np.float32(bf16(centre)))
    second_z = second_z + (centre - coarse) * np.eye(Z, dtype=np.float32)
    second_y = second_y + coarse * np.eye(Y, dtype=np.float32)
    wz_first = np.concatenate([first_z.T, first_z.T], axis=0).astype(bf16)
    wz_second = np.kron(np.eye(2, dtype=np.float32), second_z.T).astype(bf16)
    group = max(1, 128 // Y)
    wy = np.kron(np.eye(group, dtype=np.float32), np.concatenate([first_y, first_y], axis=1)).astype(bf16)
    block = rows
    wxy = np.zeros((block, Y, block + 2 * REACH, Y), np.float32)
    for x in range(block):
        wxy[x, :, x + REACH, :] = second_y
        for k in range(1, REACH + 1):
            wxy[x, :, x + REACH + k, :] = SECOND_WHOLE[k - 1] * np.eye(Y, dtype=np.float32)
            wxy[x, :, x + REACH - k, :] = SECOND_WHOLE[k - 1] * np.eye(Y, dtype=np.float32)
    wxy = wxy.reshape(block * Y, (block + 2 * REACH) * Y).astype(bf16)

    def hold(n):
        return pltpu.VMEM((fields, n, Y, Z), jnp.float32)

    soft = pltpu.VMEM(((X + 2 * REACH) * Y, (fields - 1) * Z), jnp.bfloat16)
    scratch = [hold(X), hold(X + 2 * REACH), soft, hold(X)]
    for reach in (5, 4, 3, 3, 2, 2, 2, 1, 1, 1, 0, 0):
        scratch.append(hold(min(X, rows + 2 * reach * REACH)))
    vmem = pl.BlockSpec(memory_space=pltpu.VMEM)
    return pl.pallas_call(
        functools.partial(levels_kernel, rows, len(near), len(far)),
        out_shape=jax.ShapeDtypeStruct((1, fields, rows, half, Z), jnp.float32),
        in_specs=[vmem] * (len(near) + len(far) + 4),
        out_specs=vmem,
        scratch_shapes=scratch,
        compiler_params=pltpu.CompilerParams(vmem_limit_bytes=VMEM_BUDGET),
    )(*near, *far, wz_first, wz_second, wy, wxy)


def gathered_body(state):
    gx, levels = lax.axis_size("gx"), lax.axis_size("level")
    level = lax.axis_index("level")
    swap = [(0, 1), (1, 0)]
    quarter = state.shape[1] // levels
    mine = lax.dynamic_slice_in_dim(state, level * quarter, quarter, axis=1)
    near, far = [state], [lax.ppermute(state, "gy", swap)]
    for ahead in range(1, gx):
        route = [((i + ahead) % gx, i) for i in range(gx)]
        first = lax.ppermute(mine, "gx", route)
        parts = [first]
        for e in range(1, levels):
            parts.append(lax.ppermute(first, "level", [(i, i ^ e) for i in range(levels)]))
        near += parts
        far.append(lax.ppermute(jnp.stack(parts), "gy", swap))
    return run_levels(near, far, gx)


def with_halo(block, sides, width):
    for axis, dim in sides:
        count = lax.axis_size(axis)
        forward = [(i, i + 1) for i in range(count - 1)]
        forward.append((count - 1, 0))
        backward = [(target, source) for source, target in forward]
        low = lax.ppermute(
            lax.slice_in_dim(block, block.shape[dim] - width, None, axis=dim), axis, forward
        )
        high = lax.ppermute(lax.slice_in_dim(block, 0, width, axis=dim), axis, backward)
        block = jnp.concatenate([low, block, high], axis=dim)
    return block


def shifted_2(block, axis, distance):
    devices = range(lax.axis_size(axis))
    route = [(i - distance, i) for i in devices if i - distance in devices]
    return lax.ppermute(block, axis, route)


def shifted(quantity, direction, offset):
    extent = quantity.shape[-3:]
    picks = [slice(4, extent[0] - 4), slice(4, extent[1] - 4), slice(4, extent[2] - 4)]
    picks[direction] = slice(4 + offset, extent[direction] - 4 + offset)
    leading = (slice(None),) * (quantity.ndim - 3)
    return quantity[leading + tuple(picks)]


def first_derivative(quantity, direction):
    total = 0.0
    for position, weight in enumerate(FIRST_COEF):
        total = total + weight * (
            shifted(quantity, direction, position + 1) - shifted(quantity, direction, -position - 1)
        )
    return total


def second_derivative_sum(quantity):
    total = 0.0
    for direction in range(3):
        total = total + SECOND_CENTER * shifted(quantity, direction, 0)
        for position, weight in enumerate(SECOND_COEF):
            total = total + weight * (
                shifted(quantity, direction, position + 1)
                + shifted(quantity, direction, -position - 1)
            )
    return total


def tendency(padded):
    specific_volume_inverse = padded[0]
    momentum = padded[1:4]
    energy = padded[4]
    velocity = momentum / specific_volume_inverse
    kinetic_energy_share = 0.5 * jnp.sum(velocity * velocity, axis=0)
    normal_stress_scalar = (GAMMA - 1.0) * (energy - specific_volume_inverse * kinetic_energy_share)
    absolute_kelvin_value = normal_stress_scalar / specific_volume_inverse
    divergence = 0.0
    for direction in range(3):
        along = velocity[direction]
        rows = [
            momentum[component] * along + (normal_stress_scalar if component == direction else 0.0)
            for component in range(3)
        ]
        flux = jnp.stack([momentum[direction]] + rows + [(energy + normal_stress_scalar) * along])
        divergence = divergence + first_derivative(flux, direction)
    viscous = SHEAR_COEFFICIENT * second_derivative_sum(velocity)
    conduction_contribution = SHEAR_COEFFICIENT * second_derivative_sum(
        kinetic_energy_share
    ) + CONDUCTIVITY * second_derivative_sum(absolute_kelvin_value)
    return jnp.concatenate(
        [
            -divergence[0:1],
            viscous - divergence[1:4],
            (conduction_contribution - divergence[4])[None],
        ],
        axis=0,
    )


def wrap_depth(field):
    return jnp.concatenate([field[:, :, :, -4:], field, field[:, :, :, :4]], axis=3)


def padded_faces(field):
    return wrap_depth(with_halo(field, (("gx", 1), ("gy", 2)), 4))


def sections_body(state):
    levels = lax.axis_size("level")
    rank = lax.axis_index("level")
    current = state
    before = jnp.zeros_like(state)
    middle = jnp.zeros_like(state)
    for section in range(STEPS + levels - 1):
        node = section - rank
        forcing = tendency(padded_faces(current))
        newest = shifted_2(forcing, "level", 1)
        quad_term = jnp.where(
            node == 0, 0.5 * (middle + newest), (8.0 * middle + 5.0 * newest - before) / 12.0
        )
        moved = current + DT * (forcing - middle + quad_term)
        active = jnp.logical_and(node >= 0, node < STEPS)
        current = jnp.where(active, moved, current)
        before = middle
        middle = newest
    return current[None]


def body(state):
    fields, rows, half, Z = state.shape
    gx, gy, levels = lax.axis_size("gx"), lax.axis_size("gy"), lax.axis_size("level")
    X, Y = rows * gx, half * gy
    need = 4 * fields * Y * Z * 15 * X
    simple = gy == 2 and levels == 4 and Z == 128 and Y % 32 == 0 and rows == 2 * REACH and rows % levels == 0 and half % 16 == 0
    if simple and gx % 2 == 0 and X <= rows + 6 * REACH and need <= VMEM_BUDGET:
        return gathered_body(state)
    return sections_body(state)


def solution(mesh):
    return jax.shard_map(
        body,
        mesh=mesh,
        in_specs=(P(None, "gx", "gy", None),),
        out_specs=P("level", None, "gx", "gy", None),
        check_vma=False,
    )
```

```python
import functools

import jax
import jax.numpy as jnp
import ml_dtypes
import numpy as np
from jax import lax
from jax.experimental import pallas as pl
from jax.experimental.pallas import tpu as pltpu
from jax.sharding import PartitionSpec as P

STEPS = 3


DT = 0.1
GAMMA = 1.4
SHEAR_COEFFICIENT = 0.1
CONDUCTIVITY = 0.1
FIRST_COEF = (4.0 / 5.0, -1.0 / 5.0, 4.0 / 105.0, -1.0 / 280.0)
SECOND_CENTER = -205.0 / 72.0
SECOND_COEF = (8.0 / 5.0, -1.0 / 5.0, 8.0 / 315.0, -1.0 / 560.0)
REACH = 4
SCALE = 5040
FIRST_WHOLE = tuple(round(w * SCALE) for w in FIRST_COEF)
SECOND_WHOLE = tuple(round(w * SCALE) for w in SECOND_COEF)
VMEM_BUDGET = 56 * 1024 * 1024
FLUX_ROWS = 8
MIDDLE = 0.07


def circulants(extent):
    first = np.zeros((extent, extent), np.float32)
    second = np.zeros((extent, extent), np.float32)
    for place in range(extent):
        for k in range(1, REACH + 1):
            first[place, (place + k) % extent] -= FIRST_WHOLE[k - 1]
            first[place, (place - k) % extent] += FIRST_WHOLE[k - 1]
            second[place, (place + k) % extent] += SECOND_WHOLE[k - 1]
            second[place, (place - k) % extent] += SECOND_WHOLE[k - 1]
    return first, second


def split(value):
    high = value.astype(jnp.bfloat16)
    low = (value - high.astype(jnp.float32)).astype(jnp.bfloat16)
    return high, low


def far_first(count):
    return sorted(range(1, count), key=lambda ahead: (-min(ahead, count - ahead), -ahead))


def levels_kernel(rows, n_near, n_far, *refs):
    near, far = refs[:n_near], refs[n_near : n_near + n_far]
    refs = refs[n_near + n_far :]
    wz_first, wz_second, wy, wxy, out = refs[:5]
    base, *held = refs[5:]
    fx, vis, part, G0, A1, A2, B1, A3, B2, C1, B3, C2, D1, C3, D2 = held
    fields, X, Y, Z = base.shape
    half = near[0].shape[2]
    level, side = lax.axis_index("level"), lax.axis_index("gy")
    own = (X - rows) // 2

    quarter = rows // 4

    def lay(value, core, ahead, e):
        at = pl.multiple_of(core * half, half)
        x = own + ahead * rows
        if e is None:
            base[:, x : x + rows, pl.ds(at, half), :] = value
        else:
            x = x + quarter * (level ^ e)
            x = jnp.where(x >= X, x - X, x)
            base[:, pl.ds(x, quarter), pl.ds(at, half), :] = value

    lay(near[0][...], side, 0, None)
    lay(far[0][...], 1 - side, 0, None)
    for e in range(4):
        for j, ahead in enumerate(far_first(X // rows)):
            lay(near[1 + e][j], side, ahead, e)
            lay(far[1 + e][j], 1 - side, ahead, e)

    def pointwise(u):
        rho, m0, m1, m2, energy = u
        inverse = 1.0 / rho
        v0, v1, v2 = m0 * inverse, m1 * inverse, m2 * inverse
        m00, m11, m22 = m0 * v0, m1 * v1, m2 * v2
        m01, m02, m12 = m0 * v1, m0 * v2, m1 * v2
        twice = m00 + m11 + m22
        p = (GAMMA - 1.0) * energy - (0.5 * (GAMMA - 1.0)) * twice
        heat = energy + p
        warm = inverse * ((0.5 * SHEAR_COEFFICIENT) * twice + CONDUCTIVITY * p) - MIDDLE
        s = SHEAR_COEFFICIENT
        g = [s * v0, s * v1, s * v2, warm]
        along_x = [m0, m00 + p, m01, m02, heat * v0]
        along_y = [m1, m01, m11 + p, m12, heat * v1]
        along_z = [m2, m02, m12, m22 + p, heat * v2]
        return along_x, along_y, along_z, g

    def flux_rows(make, first, count, whole):
        batch = min(FLUX_ROWS, count)

        def produce(x):
            u = [make(f, x, batch).reshape(batch * Y, Z) for f in range(fields)]
            along_x, along_y, along_z, g = pointwise(u)
            for f in range(fields):
                fx[f, pl.ds(x + REACH, batch)] = along_x[f].reshape(batch, Y, Z)
            g = jnp.concatenate([v.astype(jnp.bfloat16) for v in g], axis=1)
            at = (x + REACH) * Y
            vis[pl.ds(at if isinstance(at, int) else pl.multiple_of(at, Y), batch * Y), :] = g
            if whole:
                zs = [split(v) for v in along_z]
                ys = [split(v) for v in along_y]
                flux = jnp.concatenate([jnp.concatenate(pair, axis=1) for pair in zs], axis=0)
                flux = jnp.dot(flux, wz_first[...], preferred_element_type=jnp.float32)
                soft = jnp.concatenate([g[:, : 2 * Z], g[:, 2 * Z :]], axis=0)
                soft = jnp.dot(soft, wz_second[...], preferred_element_type=jnp.float32)
                group = wy.shape[0] // Y
                deeps = []
                for r in range(0, batch, group):
                    columns = []
                    for f in range(fields):
                        cuts = [slice((r + q) * Y, (r + q + 1) * Y) for q in range(group)]
                        columns.append(jnp.concatenate([v[cut] for cut in cuts for v in ys[f]], axis=0))
                    columns = jnp.concatenate(columns, axis=1)
                    deeps.append(jnp.dot(wy[...], columns, preferred_element_type=jnp.float32))
                return flux, soft, deeps
            return None

        def keep(x, flux, soft, deeps):
            group = wy.shape[0] // Y
            for r in range(0, batch, group):
                deep = deeps[r // group]
                for f in range(fields):
                    at = f * batch * Y + r * Y
                    total = deep[:, f * Z : (f + 1) * Z] + flux[at : at + group * Y]
                    if f:
                        at = ((f - 1) // 2) * batch * Y + r * Y
                        lane = ((f - 1) % 2) * Z
                        total = total + soft[at : at + group * Y, lane : lane + Z]
                    part[f, pl.ds(x + r, group)] = total.reshape(group, Y, Z)

        def step(i, carry):
            made = [(x, produce(x)) for x in (first + i * count + j for j in range(0, count, batch))]
            for x, values in made:
                if values:
                    keep(x, *values)
            return carry

        lax.fori_loop(0, 1, step, 0)

    def stencil_rows(target, shift, first, count):
        block = wxy.shape[0] // Y

        def soften(x):
            g = [vis[x * Y : (x + block + 2 * REACH) * Y, 2 * p * Z : 2 * (p + 1) * Z] for p in range(2)]
            return [jnp.dot(wxy[...], v, preferred_element_type=jnp.float32).reshape(block, Y, 2 * Z) for v in g]

        def end(x, soft):
            for f in range(fields):
                for y in range(0, Y, 8):
                    flux = fx[f, x : x + block + 2 * REACH, y : y + 8, :]
                    total = part[f, x : x + block, y : y + 8, :]
                    if f:
                        pair, place = divmod(f - 1, 2)
                        total = total + soft[pair][:, y : y + 8, place * Z : (place + 1) * Z]
                    for k in range(1, REACH + 1):
                        ahead = slice(REACH + k, REACH + k + block)
                        behind = slice(REACH - k, REACH - k + block)
                        total = total + float(FIRST_WHOLE[k - 1]) * (flux[behind] - flux[ahead])
                    target[f, x - shift : x - shift + block, y : y + 8, :] = (DT / SCALE) * total

        places = range(first, first + count, block)
        soft = soften(places[0])
        for x in places:
            following = soften(x + block) if x + block < first + count else None
            end(x, soft)
            soft = following

    def tendency(target, make, reach):
        first, count = own - reach, rows + 2 * reach
        if count >= X:
            first, count = 0, X
            flux_rows(make, 0, X, True)
            edge = REACH * Y
            fx[:, :REACH] = fx[:, X : X + REACH]
            fx[:, X + REACH :] = fx[:, REACH : 2 * REACH]
            vis[:edge] = vis[X * Y : X * Y + edge]
            vis[X * Y + edge :] = vis[edge : 2 * edge]
        else:
            flux_rows(make, first, count, True)
            flux_rows(make, first - REACH, REACH, False)
            flux_rows(make, first + count, REACH, False)
        stencil_rows(target, first, first, count)

    def rows_of(ref, f, x, n):
        return ref[f, pl.ds(x - (X - ref.shape[1]) // 2, n)]

    half_step, five, sixth, twelfth = 0.5, 5.0 / 12.0, 1.0 / 6.0, 1.0 / 12.0

    def mix(*terms):
        def make(f, x, n):
            total = None
            for weight, *held in terms:
                value = rows_of(held[0], f, x, n)
                for ref in held[1:]:
                    value = value + rows_of(ref, f, x, n)
                value = value if weight == 1 else weight * value
                total = value if total is None else total + value
            return total

        return make

    def second(g, low, mid, high):
        return mix((1, base, mid), (five, g, high), (sixth, low))

    u03 = ((1, base, G0, A1, A2),)
    u13 = ((1, base, B1, B2), (five, G0, A3), (twelfth, A1, A2))
    u23 = ((1, base, C1, C2), (five, G0, B3), (twelfth, B1, B2))
    u33 = ((1, base, D1, D2), (five, G0, C3), (twelfth, C1, C2))

    tendency(G0, mix((1, base)), 5 * REACH)
    tendency(A1, mix((1, base, G0)), 4 * REACH)
    tendency(A2, mix((1, base, G0, A1)), 3 * REACH)
    tendency(B1, mix((1, base), (half_step, G0, A1)), 3 * REACH)
    tendency(A3, mix(*u03), 2 * REACH)
    tendency(B2, second(G0, A1, B1, A2), 2 * REACH)
    tendency(C1, mix((1, base), (half_step, G0, B1)), 2 * REACH)
    tendency(B3, mix(*u13), REACH)
    tendency(C2, second(G0, B1, C1, B2), REACH)
    tendency(D1, mix((1, base), (half_step, G0, C1)), REACH)
    tendency(C3, mix(*u23), 0)
    tendency(D2, second(G0, C1, D1, C2), 0)

    at = pl.multiple_of(side * half, half)
    for p, terms in enumerate((u03, u13, u23, u33)):

        @pl.when(level == p)
        def _():
            for f in range(fields):
                total = None
                for weight, *held in terms:
                    value = None
                    for ref in held:
                        start = own - (X - ref.shape[1]) // 2
                        here = ref[f, start : start + rows, pl.ds(at, half), :]
                        value = here if value is None else value + here
                    value = value if weight == 1 else weight * value
                    total = value if total is None else total + value
                out[0, f] = total


def run_levels(near, far, gx):
    fields, rows, half, Z = near[0].shape
    X, Y = rows * gx, 2 * half
    bf16 = ml_dtypes.bfloat16
    first_z, second_z = circulants(Z)
    first_y, second_y = circulants(Y)
    centre = round(3 * SECOND_CENTER * SCALE)
    coarse = int(np.float32(bf16(centre)))
    second_z = second_z + (centre - coarse) * np.eye(Z, dtype=np.float32)
    second_y = second_y + coarse * np.eye(Y, dtype=np.float32)
    wz_first = np.concatenate([first_z.T, first_z.T], axis=0).astype(bf16)
    wz_second = np.kron(np.eye(2, dtype=np.float32), second_z.T).astype(bf16)
    group = max(1, 128 // Y)
    wy = np.kron(np.eye(group, dtype=np.float32), np.concatenate([first_y, first_y], axis=1)).astype(bf16)
    block = rows
    wxy = np.zeros((block, Y, block + 2 * REACH, Y), np.float32)
    for x in range(block):
        wxy[x, :, x + REACH, :] = second_y
        for k in range(1, REACH + 1):
            wxy[x, :, x + REACH + k, :] = SECOND_WHOLE[k - 1] * np.eye(Y, dtype=np.float32)
            wxy[x, :, x + REACH - k, :] = SECOND_WHOLE[k - 1] * np.eye(Y, dtype=np.float32)
    wxy = wxy.reshape(block * Y, (block + 2 * REACH) * Y).astype(bf16)

    def hold(n):
        return pltpu.VMEM((fields, n, Y, Z), jnp.float32)

    soft = pltpu.VMEM(((X + 2 * REACH) * Y, (fields - 1) * Z), jnp.bfloat16)
    scratch = [hold(X), hold(X + 2 * REACH), soft, hold(X)]
    for reach in (5, 4, 3, 3, 2, 2, 2, 1, 1, 1, 0, 0):
        scratch.append(hold(min(X, rows + 2 * reach * REACH)))
    vmem = pl.BlockSpec(memory_space=pltpu.VMEM)
    return pl.pallas_call(
        functools.partial(levels_kernel, rows, len(near), len(far)),
        out_shape=jax.ShapeDtypeStruct((1, fields, rows, half, Z), jnp.float32),
        in_specs=[vmem] * (len(near) + len(far) + 4),
        out_specs=vmem,
        scratch_shapes=scratch,
        compiler_params=pltpu.CompilerParams(vmem_limit_bytes=VMEM_BUDGET),
    )(*near, *far, wz_first, wz_second, wy, wxy)


def gathered_body(state):
    gx, levels = lax.axis_size("gx"), lax.axis_size("level")
    level = lax.axis_index("level")
    swap = [(0, 1), (1, 0)]
    quarter = state.shape[1] // levels
    mine = lax.dynamic_slice_in_dim(state, level * quarter, quarter, axis=1)
    far = [lax.ppermute(state, "gy", swap)]
    first = []
    for ahead in far_first(gx):
        first.append(lax.ppermute(mine, "gx", [((i + ahead) % gx, i) for i in range(gx)]))
    first = jnp.stack(first)
    parts = {0: first}
    for e in range(levels - 1, 0, -1):
        parts[e] = lax.ppermute(first, "level", [(i, i ^ e) for i in range(levels)])
    swapped = {e: lax.ppermute(part, "gy", swap) for e, part in parts.items()}
    near = [state] + [parts[e] for e in range(levels)]
    far += [swapped[e] for e in range(levels)]
    return run_levels(near, far, gx)


def with_halo(block, sides, width):
    for axis, dim in sides:
        count = lax.axis_size(axis)
        forward = [(i, i + 1) for i in range(count - 1)]
        forward.append((count - 1, 0))
        backward = [(target, source) for source, target in forward]
        low = lax.ppermute(
            lax.slice_in_dim(block, block.shape[dim] - width, None, axis=dim), axis, forward
        )
        high = lax.ppermute(lax.slice_in_dim(block, 0, width, axis=dim), axis, backward)
        block = jnp.concatenate([low, block, high], axis=dim)
    return block


def shifted_2(block, axis, distance):
    devices = range(lax.axis_size(axis))
    route = [(i - distance, i) for i in devices if i - distance in devices]
    return lax.ppermute(block, axis, route)


def shifted(quantity, direction, offset):
    extent = quantity.shape[-3:]
    picks = [slice(4, extent[0] - 4), slice(4, extent[1] - 4), slice(4, extent[2] - 4)]
    picks[direction] = slice(4 + offset, extent[direction] - 4 + offset)
    leading = (slice(None),) * (quantity.ndim - 3)
    return quantity[leading + tuple(picks)]


def first_derivative(quantity, direction):
    total = 0.0
    for position, weight in enumerate(FIRST_COEF):
        total = total + weight * (
            shifted(quantity, direction, position + 1) - shifted(quantity, direction, -position - 1)
        )
    return total


def second_derivative_sum(quantity):
    total = 0.0
    for direction in range(3):
        total = total + SECOND_CENTER * shifted(quantity, direction, 0)
        for position, weight in enumerate(SECOND_COEF):
            total = total + weight * (
                shifted(quantity, direction, position + 1)
                + shifted(quantity, direction, -position - 1)
            )
    return total


def tendency(padded):
    specific_volume_inverse = padded[0]
    momentum = padded[1:4]
    energy = padded[4]
    velocity = momentum / specific_volume_inverse
    kinetic_energy_share = 0.5 * jnp.sum(velocity * velocity, axis=0)
    normal_stress_scalar = (GAMMA - 1.0) * (energy - specific_volume_inverse * kinetic_energy_share)
    absolute_kelvin_value = normal_stress_scalar / specific_volume_inverse
    divergence = 0.0
    for direction in range(3):
        along = velocity[direction]
        rows = [
            momentum[component] * along + (normal_stress_scalar if component == direction else 0.0)
            for component in range(3)
        ]
        flux = jnp.stack([momentum[direction]] + rows + [(energy + normal_stress_scalar) * along])
        divergence = divergence + first_derivative(flux, direction)
    viscous = SHEAR_COEFFICIENT * second_derivative_sum(velocity)
    conduction_contribution = SHEAR_COEFFICIENT * second_derivative_sum(
        kinetic_energy_share
    ) + CONDUCTIVITY * second_derivative_sum(absolute_kelvin_value)
    return jnp.concatenate(
        [
            -divergence[0:1],
            viscous - divergence[1:4],
            (conduction_contribution - divergence[4])[None],
        ],
        axis=0,
    )


def wrap_depth(field):
    return jnp.concatenate([field[:, :, :, -4:], field, field[:, :, :, :4]], axis=3)


def padded_faces(field):
    return wrap_depth(with_halo(field, (("gx", 1), ("gy", 2)), 4))


def sections_body(state):
    levels = lax.axis_size("level")
    rank = lax.axis_index("level")
    current = state
    before = jnp.zeros_like(state)
    middle = jnp.zeros_like(state)
    for section in range(STEPS + levels - 1):
        node = section - rank
        forcing = tendency(padded_faces(current))
        newest = shifted_2(forcing, "level", 1)
        quad_term = jnp.where(
            node == 0, 0.5 * (middle + newest), (8.0 * middle + 5.0 * newest - before) / 12.0
        )
        moved = current + DT * (forcing - middle + quad_term)
        active = jnp.logical_and(node >= 0, node < STEPS)
        current = jnp.where(active, moved, current)
        before = middle
        middle = newest
    return current[None]


def body(state):
    fields, rows, half, Z = state.shape
    gx, gy, levels = lax.axis_size("gx"), lax.axis_size("gy"), lax.axis_size("level")
    X, Y = rows * gx, half * gy
    need = 4 * fields * Y * Z * 15 * X
    simple = gy == 2 and levels == 4 and Z == 128 and Y % 32 == 0 and rows == 2 * REACH and rows % levels == 0 and half % 16 == 0
    if simple and gx % 2 == 0 and X <= rows + 6 * REACH and need <= VMEM_BUDGET:
        return gathered_body(state)
    return sections_body(state)


def solution(mesh):
    return jax.shard_map(
        body,
        mesh=mesh,
        in_specs=(P(None, "gx", "gy", None),),
        out_specs=P("level", None, "gx", "gy", None),
        check_vma=False,
    )
```
